32 devices in a mesh: groups: 1, nodes: 16 (over z, y, core), local: 2 (over x).
Axes of the slice: x: 2, y: 2, z: 4, core: 2. Of those that a mesh axis runs over, the one named last changes fastest.
Arguments:
- hidden_in: bfloat16 [256, 3584], P(('groups', 'nodes', 'local')), may hold values from -6 to 6
- queries: bfloat16 [256, 64, 576], P(('groups', 'nodes', 'local')), may hold values from -100 to 100
- cache: bfloat16 [256, 128, 576], P(('groups', 'nodes', 'local')), may hold values from -6 to 6
- lengths: int32 [256], P(('groups', 'nodes', 'local')), may hold values from 2 to 128, as said below
- expert_ids: int32 [256, 8], P(('groups', 'nodes', 'local')), may hold values from 0 to 15, all different within a row; in each aligned block of 4 rows (0 to 3, 4 to 7, ...) at most 4 rows name the same one
- gate_weights: float32 [256, 8], P(('groups', 'nodes', 'local')), may hold values from 0.1 to 1
- w_gate: bfloat16 [16, 3584, 1024], P('nodes', None, 'local'), may hold values from -0.09375 to 0.09375
- w_up: bfloat16 [16, 3584, 1024], P('nodes', None, 'local'), may hold values from -0.09375 to 0.09375
- w_down: bfloat16 [16, 1024, 3584], P('nodes', 'local'), may hold values from -0.1875 to 0.1875
Outputs:
- context: bfloat16 [256, 32768], P(('groups', 'nodes', 'local'))
- expert_out: bfloat16 [256, 3584], P(('groups', 'nodes', 'local'))
The draws below stay inside these ranges and needn't reach their ends.
Inputs may be any that keep to these rules, and one draw needn't show every extreme that they name: `lengths`: each row has at least two live positions; in every part some row has all 128. `expert_ids`: ids of a row are distinct; in each aligned block of 4 rows no expert is named more than 4 times.
All inputs are finite; a program needn't handle non-finite values.
Results may differ from the reference program's by a relative error of at most 0.012.
Values may be sent and summed in bfloat16 or wider, within the bound.
No kernel may reach another device: no remote copies, remote signals or barrier semaphores. Data moves between devices by JAX's collectives and lax.ppermute only.
A program may use at most 64 MiB of HBM per device.

```python
import math
import jax
import jax.numpy as jnp
import numpy as np
from jax import lax

D = 3584
FFN = 1024
HEADS = 64
LATENT = 512
ROPE = 64
TOP = 8
ROWS_MB = 4
LEN = 128
EXPERTS = 16
CAP = 4
TOKENS = 256
N_LOCAL = 2


def shared_cache(key):
    return jnp.clip(jax.random.normal(key, (TOKENS, LEN, LATENT + ROPE), jnp.float32), -6.0, 6.0)


def draw_cache(key, part):
    return shared_cache(key).astype(jnp.bfloat16)


def draw_queries(key, part):
    key = jax.random.fold_in(key, 5)
    noise = jax.random.normal(key, (TOKENS, HEADS, LATENT + ROPE), jnp.float32)
    return jnp.clip(noise, -100.0, 100.0).astype(jnp.bfloat16)


def draw_lengths(key, part):
    key = jax.random.fold_in(key, 7)
    drawn = jax.random.randint(key, (TOKENS,), 2, LEN + 1)
    return drawn.at[0].set(LEN).astype(jnp.int32)


def level_of(rng, shape, split, low, largest):
    gain = 1.0
    for position, parts in split:
        heights = jax.random.uniform(jax.random.fold_in(jax.random.fold_in(rng, 6), position), (parts,), jnp.float32, low / len(split), largest / len(split))
        gain = gain * jnp.repeat(jnp.exp(heights), shape[position] // parts).reshape((-1,) + (1,) * (len(shape) - 1 - position))
    return gain


def deal_out(own_key, own, number, rows, number_of, top, most, lean):
    order = jax.random.permutation(own_key, number_of)
    packed, common = load_shares(number_of, rows * top, most, lean, True), load_shares(number_of, rows * top, most, lean, False)
    places = jnp.arange(number_of)

    def named(sizes, offset_by):
        used = int((sizes > 0).sum())
        fixed = max(1, used // 4)
        shifted = fixed + (places - fixed + offset_by * (used - fixed)) % max(1, number_of - fixed)
        return jnp.zeros((number_of,), jnp.int32).at[order[jnp.where(places < fixed, places, shifted)]].set(jnp.asarray(sizes, jnp.int32))

    sizes = jnp.where(number % 4 == 0, named(packed, number // 4), named(common, number - number // 4 - 1))
    mixed = jax.random.permutation(jax.random.fold_in(own, 3), number_of)
    giver, taker = mixed[0:number_of // 2 * 2:2], mixed[1:number_of // 2 * 2:2]
    room = jnp.minimum(sizes[giver] - 1, most - sizes[taker]) // 2
    room = jnp.where((giver == order[0]) | (taker == order[0]) | (sizes[taker] == 0), 0, jnp.maximum(room, 0))
    shifted = jax.random.randint(jax.random.fold_in(own, 4), (number_of // 2,), 0, 1 << 20) % (room + 1)
    sizes = sizes.at[giver].add(-shifted).at[taker].add(shifted)
    members = jnp.searchsorted(jnp.cumsum(sizes), jnp.arange(rows * top), side="right").astype(jnp.int32)
    listing = members.reshape(top, rows).T
    listing = listing[jax.random.permutation(jax.random.fold_in(own, 1), rows)]
    offset_by = jax.random.randint(jax.random.fold_in(own, 2), (rows, 1), 0, top)
    return jnp.take_along_axis(listing, (jnp.arange(top)[None, :] + offset_by) % top, axis=1)


def load_shares(amount, total, bound, slope, full):
    portions = [(1 << 20) // math.isqrt(grade ** slope) + 1 for grade in range(1, amount + 1)]
    largest = bound if full else min(bound, max(-(-total // amount), total * portions[0] // sum(portions)))
    least = 1 if total - largest >= amount - 1 else 0
    given, rest = [largest] + [least] * (amount - 1), total - largest - least * (amount - 1)
    while rest > 0:
        free = [i for i in range(1, amount) if given[i] < largest] or [i for i in range(1, amount) if given[i] < bound]
        whole, budget = sum([portions[i] for i in free]), rest
        for i in free:
            more = min(bound - given[i], max(1, budget * portions[i] // whole), rest)
            given[i] = given[i] + more
            rest = rest - more
    return np.array(given)


def centred(rng, extent, scale, limit, shards=(), kind=jnp.bfloat16):
    values = jax.random.normal(rng, extent, jnp.float32) * scale
    if len(shards) > 0:
        values = level_of(rng, extent, shards, -0.22, 0.18) * values
    return jnp.clip(values, min=-limit, max=limit).astype(kind)


def setup_inputs(seed: int = 0, part: int = 0) -> dict:
    key_list = jax.random.split(jax.random.key(seed), 10)
    part_splits = jax.random.split(jax.random.fold_in(key_list[9], part), 10)
    hidden_in = centred(part_splits[0], (TOKENS, D), 1.0, 6.0, ((0, 32),))
    queries = draw_queries(jax.random.fold_in(jax.random.fold_in(key_list[9], part), 71), part)
    cache = draw_cache(jax.random.fold_in(jax.random.fold_in(key_list[9], part), 71), part)
    lengths = draw_lengths(jax.random.fold_in(jax.random.fold_in(key_list[9], part), 71), part)
    expert_ids_keys = jax.random.split(jax.random.fold_in(part_splits[4], 1), TOKENS // ROWS_MB)
    expert_ids_turns = jax.random.permutation(jax.random.fold_in(part_splits[4], 3), TOKENS // ROWS_MB)
    expert_ids = jax.vmap(lambda own, number: deal_out(jax.random.fold_in(part_splits[4], 2), own, number, ROWS_MB, EXPERTS, TOP, CAP, 2))(expert_ids_keys, expert_ids_turns).reshape((TOKENS, TOP))
    gate_weights = jnp.clip(jnp.exp(math.log(1.0) - 2.3025851 * jax.random.uniform(part_splits[5], (TOKENS, TOP), jnp.float32) ** level_of(part_splits[5], (TOKENS, TOP), ((0, 32),), -0.2, 0.2)), 0.1, 1.0)
    w_gate = centred(key_list[6], (EXPERTS, D, FFN), D ** -0.5, 0.09375, ((0, 16), (2, 2)))
    w_up = centred(key_list[7], (EXPERTS, D, FFN), D ** -0.5, 0.09375, ((0, 16), (2, 2)))
    w_down = centred(key_list[8], (EXPERTS, FFN, D), FFN ** -0.5, 0.1875, ((0, 16), (1, 2)))
    return {"hidden_in": hidden_in, "queries": queries, "cache": cache, "lengths": lengths, "expert_ids": expert_ids, "gate_weights": gate_weights, "w_gate": w_gate, "w_up": w_up, "w_down": w_down}


softmax_scale = 0.0722


def reference(hidden_in, queries, cache, lengths, expert_ids, gate_weights, w_gate, w_up, w_down):
    query_f = queries.astype(jnp.float32)
    cache_f = cache.astype(jnp.float32)
    scores = jnp.einsum('bhd,btd->bht', query_f, cache_f) * softmax_scale
    valid = lax.broadcasted_iota(jnp.int32, (1, 1, LEN), 2) < lengths[:, None, None]
    scores = jnp.where(valid, scores, -1e30)
    highest = jnp.max(scores, axis=-1, keepdims=True)
    expo = jnp.exp(scores - highest)
    probs = (expo / jnp.sum(expo, axis=-1, keepdims=True)).astype(jnp.bfloat16)
    context = jnp.einsum('bht,btc->bhc', probs.astype(jnp.float32), cache_f[:, :, :LATENT])
    context = context.astype(jnp.bfloat16).reshape(TOKENS, HEADS * LATENT)

    blocks = TOKENS // ROWS_MB
    pairs = ROWS_MB * TOP
    block_ids = expert_ids.reshape(blocks, pairs)
    onehot = (block_ids[:, :, None] == jnp.arange(EXPERTS, dtype=jnp.int32)[None, None, :]).astype(jnp.int32)
    earlier = jnp.cumsum(onehot, axis=1) - onehot
    slots = jnp.sum(earlier * onehot, axis=2).astype(jnp.int32)
    block_index = jnp.broadcast_to(jnp.arange(blocks, dtype=jnp.int32)[:, None], (blocks, pairs))
    token_index = (block_index * ROWS_MB + jnp.arange(pairs, dtype=jnp.int32)[None, :] // TOP).astype(jnp.int32)
    flat_e = block_ids.reshape(-1)
    flat_b = block_index.reshape(-1)
    flat_s = slots.reshape(-1)
    flat_t = token_index.reshape(-1)
    buffer = jnp.zeros((EXPERTS, blocks, CAP, D), jnp.bfloat16)
    buffer = buffer.at[flat_e, flat_b, flat_s].set(hidden_in[flat_t])

    def one_expert(args):
        rows, gate_w, up_w, down_w = args
        rows = rows.reshape(blocks * CAP, D)
        gate = jnp.dot(rows, gate_w, preferred_element_type=jnp.float32)
        upper = jnp.dot(rows, up_w, preferred_element_type=jnp.float32)
        act = (jax.nn.silu(gate) * upper).astype(jnp.bfloat16)
        pieces = act.reshape(blocks * CAP, N_LOCAL, FFN // N_LOCAL).astype(jnp.float32)
        down_pieces = down_w.reshape(N_LOCAL, FFN // N_LOCAL, D).astype(jnp.float32)
        partial_value = jnp.einsum('rlf,lfd->lrd', pieces, down_pieces).astype(jnp.bfloat16)
        total = jnp.sum(partial_value.astype(jnp.float32), axis=0).astype(jnp.bfloat16)
        return total.reshape(blocks, CAP, D)

    values = lax.map(one_expert, (buffer, w_gate, w_up, w_down))
    picked = values[flat_e, flat_b, flat_s].astype(jnp.float32).reshape(TOKENS, TOP, D)
    expert_out = jnp.sum(gate_weights[:, :, None] * picked, axis=1).astype(jnp.bfloat16)
    return context, expert_out
```

```python
import jax
import jax.numpy as jnp
from jax import lax
from jax.experimental import pallas as pl
from jax.experimental.pallas import tpu as pltpu
from jax.sharding import Mesh, PartitionSpec as P

LATENT = 512
LANES = 128
TERMS = 3

softmax_scale = 0.0722


def attend(queries, cache, lengths):
    scores = (
        jnp.einsum("bhd,btd->bht", queries, cache, preferred_element_type=jnp.float32)
        * softmax_scale
    )
    valid = lax.broadcasted_iota(jnp.int32, (1, 1, cache.shape[1]), 2) < lengths[:, None, None]
    scores = jnp.where(valid, scores, -1e30)
    highest = jnp.max(scores, axis=-1, keepdims=True)
    expo = jnp.exp(scores - highest)
    probs = (expo / jnp.sum(expo, axis=-1, keepdims=True)).astype(jnp.bfloat16)
    context = jnp.einsum(
        "bht,btc->bhc", probs, cache[:, :, :LATENT], preferred_element_type=jnp.float32
    )
    return context.astype(jnp.bfloat16).reshape(queries.shape[0], queries.shape[1] * LATENT)


def pack_kernel(experts, hidden_ref, ids_ref, weights_ref, out_ref):
    rows, width = hidden_ref.shape
    extra = out_ref.shape[1] - width
    out_ref[:, :width] = hidden_ref[...]
    lane = lax.broadcasted_iota(jnp.int32, (rows, extra), 1)
    expert, term = lane % experts, lane // experts
    dense = jnp.zeros((rows, extra), jnp.float32)
    for k in range(ids_ref.shape[1]):
        dense = dense + jnp.where(ids_ref[:, k : k + 1] == expert, weights_ref[:, k : k + 1], 0.0)
    high = dense.astype(jnp.bfloat16).astype(jnp.float32)
    rest = dense - high
    middle = rest.astype(jnp.bfloat16).astype(jnp.float32)
    low = rest - middle
    terms = jnp.where(term == 0, high, jnp.where(term == 1, middle, low))
    out_ref[:, width:] = jnp.where(term < TERMS, terms, 0.0).astype(jnp.bfloat16)


def pack(hidden, ids, weights, experts):
    rows, width = hidden.shape
    extra = -(-experts * TERMS // LANES) * LANES
    return pl.pallas_call(
        lambda *refs: pack_kernel(experts, *refs),
        out_shape=jax.ShapeDtypeStruct((rows, width + extra), jnp.bfloat16),
        name="pack",
    )(hidden, ids, weights)


def expert_kernel(experts, chunk, me_ref, mine_ref, other_ref, gate_hbm, up_hbm, down_hbm, mine_out, other_out, rows_ref, gate_w, up_w, down_w, gate_acc, up_acc, sems):
    half = mine_ref.shape[0]
    width = mine_out.shape[1]
    units = gate_w.shape[1]
    steps = width // chunk
    copies = []
    for k in range(steps):
        part = pl.ds(k * chunk, chunk)
        copies.append(pltpu.make_async_copy(gate_hbm.at[part], gate_w.at[part], sems.at[0, k]))
        copies.append(pltpu.make_async_copy(up_hbm.at[part], up_w.at[part], sems.at[1, k]))
    for k in range(steps):
        part = pl.ds(k * chunk, chunk)
        copies.append(pltpu.make_async_copy(down_hbm.at[:, part], down_w.at[:, part], sems.at[2, k]))
    for copy in copies:
        copy.start()
    rows_ref[:half] = mine_ref[...]
    rows_ref[half:] = other_ref[...]
    for k in range(steps):
        copies[2 * k].wait()
        copies[2 * k + 1].wait()
        piece = rows_ref[:, k * chunk : (k + 1) * chunk]
        gate = jnp.dot(piece, gate_w[k * chunk : (k + 1) * chunk], preferred_element_type=jnp.float32)
        up = jnp.dot(piece, up_w[k * chunk : (k + 1) * chunk], preferred_element_type=jnp.float32)
        if k == 0:
            gate_acc[...] = gate
            up_acc[...] = up
        else:
            gate_acc[...] += gate
            up_acc[...] += up
    gate = gate_acc[...]
    act = (gate / (1.0 + jnp.exp(-gate)) * up_acc[...]).astype(jnp.bfloat16)
    info = rows_ref[:, width:].astype(jnp.float32)
    lane = lax.broadcasted_iota(jnp.int32, info.shape, 1)
    me = me_ref[0]
    mask = (lane == me) | (lane == me + experts) | (lane == me + 2 * experts)
    weight = jnp.sum(jnp.where(mask, info, 0.0), axis=1, keepdims=True)
    for k in range(steps):
        copies[2 * steps + k].wait()
        value = jnp.dot(act, down_w[:, k * chunk : (k + 1) * chunk], preferred_element_type=jnp.float32)
        value = (value * weight).astype(jnp.bfloat16)
        mine_out[:, k * chunk : (k + 1) * chunk] = value[:half]
        other_out[:, k * chunk : (k + 1) * chunk] = value[half:]


def expert_values(mine, other, w_gate, w_up, w_down, experts):
    half, packed = mine.shape
    width, units = w_gate.shape
    chunk = 512
    steps = width // chunk
    me = (lax.axis_index(("z1", "mid", "core"))).astype(jnp.int32).reshape(1)
    vmem = pl.BlockSpec(memory_space=pltpu.VMEM)
    hbm = pl.BlockSpec(memory_space=pl.ANY)
    out = jax.ShapeDtypeStruct((half, width), jnp.bfloat16)
    return pl.pallas_call(
        lambda *refs: expert_kernel(experts, chunk, *refs),
        out_shape=(out, out),
        in_specs=[pl.BlockSpec(memory_space=pltpu.SMEM), vmem, vmem, hbm, hbm, hbm],
        out_specs=(vmem, vmem),
        scratch_shapes=[
            pltpu.VMEM((2 * half, packed), jnp.bfloat16),
            pltpu.VMEM((width, units), jnp.bfloat16),
            pltpu.VMEM((width, units), jnp.bfloat16),
            pltpu.VMEM((units, width), jnp.bfloat16),
            pltpu.VMEM((2 * half, units), jnp.float32),
            pltpu.VMEM((2 * half, units), jnp.float32),
            pltpu.SemaphoreType.DMA((3, steps)),
        ],
        compiler_params=pltpu.CompilerParams(vmem_limit_bytes=60 * 1024 * 1024),
        cost_estimate=pl.CostEstimate(
            flops=2 * 2 * half * width * units * 3,
            bytes_accessed=3 * width * units * 2 + 4 * half * packed * 2,
            transcendentals=2 * half * units,
        ),
        name="expert",
    )(me, mine, other, w_gate, w_up, w_down)


def routed_layer(hidden, ids, weights, w_gate, w_up, w_down):
    rows, width = hidden.shape
    block = lax.axis_size("mid") * lax.axis_size("local")
    experts = w_gate.shape[0] * lax.axis_size("z1") * lax.axis_size("mid") * lax.axis_size("core")
    swap = [(0, 1), (1, 0)]
    packed = pack(hidden, ids, weights, experts)
    far = lax.ppermute(packed, "z1", swap)
    pair = jnp.concatenate([packed, far], axis=0)
    sending = jnp.broadcast_to(pair[None], (block,) + pair.shape)
    mine = lax.all_to_all(sending, ("mid", "local"), split_axis=0, concat_axis=0, tiled=True)
    mine = mine.reshape(block * 2 * rows, packed.shape[1])
    other = lax.ppermute(mine, "core", swap)
    mine_out, other_out = expert_values(mine, other, w_gate[0], w_up[0], w_down[0], experts)
    from_other = lax.ppermute(other_out, "core", swap)
    total = (mine_out.astype(jnp.float32) + from_other.astype(jnp.float32)).astype(jnp.bfloat16)
    back = lax.all_to_all(
        total.reshape(block, 2 * rows, width), ("mid", "local"), split_axis=0, concat_axis=0, tiled=True
    )
    back = jnp.sum(back.astype(jnp.float32), axis=0)
    for_far = back[rows:].astype(jnp.bfloat16)
    from_far = lax.ppermute(for_far, "z1", swap)
    return (back[:rows] + from_far.astype(jnp.float32)).astype(jnp.bfloat16)


def on_device(hidden_in, queries, cache, lengths, expert_ids, gate_weights, w_gate, w_up, w_down):
    expert_out = routed_layer(hidden_in, expert_ids, gate_weights, w_gate, w_up, w_down)
    context = attend(queries, cache, lengths)
    return (context, expert_out)


def solution(mesh):
    groups, nodes, local = mesh.shape["groups"], mesh.shape["nodes"], mesh.shape["local"]
    fine = Mesh(
        mesh.devices.reshape(groups, 2, nodes // 4, 2, local),
        ("groups", "z1", "mid", "core", "local"),
    )
    every = ("groups", "z1", "mid", "core", "local")
    nodes = ("z1", "mid", "core")
    return jax.shard_map(
        on_device,
        mesh=fine,
        in_specs=(
            P(every, None),
            P(every, None, None),
            P(every, None, None),
            P(every),
            P(every, None),
            P(every, None),
            P(nodes, None, "local"),
            P(nodes, None, "local"),
            P(nodes, "local", None),
        ),
        out_specs=(P(every, None), P(every, None)),
        check_vma=False,
    )
```

```python
import jax
import jax.numpy as jnp
from jax import lax
from jax.experimental import pallas as pl
from jax.experimental.pallas import tpu as pltpu
from jax.sharding import Mesh, PartitionSpec as P

LATENT = 512
LANES = 128
TERMS = 3

softmax_scale = 0.0722


def attend(queries, cache, lengths):
    scores = (
        jnp.einsum("bhd,btd->bht", queries, cache, preferred_element_type=jnp.float32)
        * softmax_scale
    )
    valid = lax.broadcasted_iota(jnp.int32, (1, 1, cache.shape[1]), 2) < lengths[:, None, None]
    scores = jnp.where(valid, scores, -1e30)
    highest = jnp.max(scores, axis=-1, keepdims=True)
    expo = jnp.exp(scores - highest)
    probs = (expo / jnp.sum(expo, axis=-1, keepdims=True)).astype(jnp.bfloat16)
    context = jnp.einsum(
        "bht,btc->bhc", probs, cache[:, :, :LATENT], preferred_element_type=jnp.float32
    )
    return context.astype(jnp.bfloat16).reshape(queries.shape[0], queries.shape[1] * LATENT)


def pack_kernel(experts, hidden_ref, ids_ref, weights_ref, out_ref):
    rows, width = hidden_ref.shape
    extra = out_ref.shape[1] - width
    out_ref[:, :width] = hidden_ref[...]
    lane = lax.broadcasted_iota(jnp.int32, (rows, extra), 1)
    expert, term = lane % experts, lane // experts
    dense = jnp.zeros((rows, extra), jnp.float32)
    for k in range(ids_ref.shape[1]):
        dense = dense + jnp.where(ids_ref[:, k : k + 1] == expert, weights_ref[:, k : k + 1], 0.0)
    high = dense.astype(jnp.bfloat16).astype(jnp.float32)
    rest = dense - high
    middle = rest.astype(jnp.bfloat16).astype(jnp.float32)
    low = rest - middle
    terms = jnp.where(term == 0, high, jnp.where(term == 1, middle, low))
    out_ref[:, width:] = jnp.where(term < TERMS, terms, 0.0).astype(jnp.bfloat16)


def pack(hidden, ids, weights, experts):
    rows, width = hidden.shape
    extra = -(-experts * TERMS // LANES) * LANES
    return pl.pallas_call(
        lambda *refs: pack_kernel(experts, *refs),
        out_shape=jax.ShapeDtypeStruct((rows, width + extra), jnp.bfloat16),
        name="pack",
    )(hidden, ids, weights)


def expert_kernel(experts, chunk, me_ref, mine_ref, other_ref, gate_w, up_w, down_w, mine_out, other_out):
    half, width = mine_out.shape
    info = jnp.concatenate([mine_ref[:, width:], other_ref[:, width:]], axis=0).astype(jnp.float32)
    lane = lax.broadcasted_iota(jnp.int32, info.shape, 1)
    me = me_ref[0]
    mask = (lane == me) | (lane == me + experts) | (lane == me + 2 * experts)
    weight = jnp.sum(jnp.where(mask, info, 0.0), axis=1, keepdims=True)
    rows = jnp.concatenate([mine_ref[:, :width], other_ref[:, :width]], axis=0)
    gate = jnp.dot(rows, gate_w[...], preferred_element_type=jnp.float32)
    up = jnp.dot(rows, up_w[...], preferred_element_type=jnp.float32)
    act = (gate / (1.0 + jnp.exp(-gate)) * up).astype(jnp.bfloat16)
    for k in range(width // chunk):
        part = slice(k * chunk, (k + 1) * chunk)
        value = jnp.dot(act, down_w[:, part], preferred_element_type=jnp.float32)
        value = (value * weight).astype(jnp.bfloat16)
        mine_out[:, part] = value[:half]
        other_out[:, part] = value[half:]


def load_kernel(gate_hbm, up_hbm, down_hbm, gate_out, up_out, down_out, sems):
    pairs = ((gate_hbm, gate_out), (up_hbm, up_out), (down_hbm, down_out))
    copies = [pltpu.make_async_copy(a, b, sems.at[i]) for i, (a, b) in enumerate(pairs)]
    for copy in copies:
        copy.start()
    for copy in copies:
        copy.wait()


def load(*matrices):
    size = sum(m.size * m.dtype.itemsize for m in matrices)
    return pl.pallas_call(
        load_kernel,
        out_shape=tuple(pltpu.VMEM(m.shape, m.dtype) for m in matrices),
        in_specs=[pl.BlockSpec(memory_space=pltpu.HBM)] * len(matrices),
        out_specs=tuple(pl.BlockSpec(memory_space=pltpu.VMEM) for _ in matrices),
        scratch_shapes=[pltpu.SemaphoreType.DMA((len(matrices),))],
        compiler_params=pltpu.CompilerParams(vmem_limit_bytes=1024 * 1024),
        cost_estimate=pl.CostEstimate(flops=0, bytes_accessed=2 * size, transcendentals=0),
        name="load",
    )(*(pltpu.with_memory_space_constraint(m, pltpu.HBM) for m in matrices))


def expert_values(mine, other, w_gate, w_up, w_down, experts):
    half, packed = mine.shape
    width, units = w_gate.shape
    me = lax.axis_index(("z1", "mid", "core")).astype(jnp.int32).reshape(1)
    vmem = pl.BlockSpec(memory_space=pltpu.VMEM)
    fast = lambda w: pltpu.with_memory_space_constraint(w, pltpu.VMEM)
    out = pltpu.VMEM((half, width), jnp.bfloat16)
    return pl.pallas_call(
        lambda *refs: expert_kernel(experts, 512, *refs),
        out_shape=(out, out),
        in_specs=[pl.BlockSpec(memory_space=pltpu.SMEM)] + [vmem] * 5,
        out_specs=(vmem, vmem),
        compiler_params=pltpu.CompilerParams(vmem_limit_bytes=12 * 1024 * 1024),
        cost_estimate=pl.CostEstimate(
            flops=2 * 2 * half * width * units * 3,
            bytes_accessed=3 * width * units * 2 + 4 * half * packed * 2,
            transcendentals=2 * half * units,
        ),
        name="expert",
    )(me, fast(mine), fast(other), fast(w_gate), fast(w_up), fast(w_down))


def routed_layer(hidden, ids, weights, w_gate, w_up, w_down):
    rows, width = hidden.shape
    block = lax.axis_size("mid") * lax.axis_size("local")
    experts = w_gate.shape[0] * lax.axis_size("z1") * lax.axis_size("mid") * lax.axis_size("core")
    swap = [(0, 1), (1, 0)]
    packed = pack(hidden, ids, weights, experts)
    far = lax.ppermute(packed, "z1", swap)
    pair = jnp.concatenate([packed, far], axis=0)
    sending = jnp.broadcast_to(pair[None], (block,) + pair.shape)
    mine = lax.all_to_all(sending, ("mid", "local"), split_axis=0, concat_axis=0, tiled=True)
    mine = mine.reshape(block * 2 * rows, packed.shape[1])
    other = lax.ppermute(mine, "core", swap)
    mine_out, other_out = expert_values(mine, other, *load(w_gate[0], w_up[0], w_down[0]), experts)
    from_other = lax.ppermute(other_out, "core", swap)
    total = (mine_out.astype(jnp.float32) + from_other.astype(jnp.float32)).astype(jnp.bfloat16)
    back = lax.all_to_all(
        total.reshape(block, 2 * rows, width), ("mid", "local"), split_axis=0, concat_axis=0, tiled=True
    )
    back = jnp.sum(back.astype(jnp.float32), axis=0)
    for_far = back[rows:].astype(jnp.bfloat16)
    from_far = lax.ppermute(for_far, "z1", swap)
    return (back[:rows] + from_far.astype(jnp.float32)).astype(jnp.bfloat16)


def on_device(hidden_in, queries, cache, lengths, expert_ids, gate_weights, w_gate, w_up, w_down):
    expert_out = routed_layer(hidden_in, expert_ids, gate_weights, w_gate, w_up, w_down)
    context = attend(queries, cache, lengths)
    return (context, expert_out)


def solution(mesh):
    groups, nodes, local = mesh.shape["groups"], mesh.shape["nodes"], mesh.shape["local"]
    fine = Mesh(
        mesh.devices.reshape(groups, 2, nodes // 4, 2, local),
        ("groups", "z1", "mid", "core", "local"),
    )
    every = ("groups", "z1", "mid", "core", "local")
    nodes = ("z1", "mid", "core")
    return jax.shard_map(
        on_device,
        mesh=fine,
        in_specs=(
            P(every, None),
            P(every, None, None),
            P(every, None, None),
            P(every),
            P(every, None),
            P(every, None),
            P(nodes, None, "local"),
            P(nodes, None, "local"),
            P(nodes, "local", None),
        ),
        out_specs=(P(every, None), P(every, None)),
        check_vma=False,
    )
```

```python
import jax
import jax.numpy as jnp
from jax import lax
from jax.experimental import pallas as pl
from jax.experimental.pallas import tpu as pltpu
from jax.sharding import PartitionSpec as P

LATENT = 512
LANES = 128
TERMS = 3

softmax_scale = 0.0722


def attend(queries, cache, lengths):
    scores = (
        jnp.einsum("bhd,btd->bht", queries, cache, preferred_element_type=jnp.float32)
        * softmax_scale
    )
    valid = lax.broadcasted_iota(jnp.int32, (1, 1, cache.shape[1]), 2) < lengths[:, None, None]
    scores = jnp.where(valid, scores, -1e30)
    highest = jnp.max(scores, axis=-1, keepdims=True)
    expo = jnp.exp(scores - highest)
    probs = (expo / jnp.sum(expo, axis=-1, keepdims=True)).astype(jnp.bfloat16)
    context = jnp.einsum(
        "bht,btc->bhc", probs, cache[:, :, :LATENT], preferred_element_type=jnp.float32
    )
    return context.astype(jnp.bfloat16).reshape(queries.shape[0], queries.shape[1] * LATENT)


def pack_kernel(experts, hidden_ref, ids_ref, weights_ref, out_ref):
    rows, width = hidden_ref.shape
    extra = out_ref.shape[1] - width
    out_ref[:, :width] = hidden_ref[...]
    lane = lax.broadcasted_iota(jnp.int32, (rows, extra), 1)
    expert, term = lane % experts, lane // experts
    dense = jnp.zeros((rows, extra), jnp.float32)
    for k in range(ids_ref.shape[1]):
        dense = dense + jnp.where(ids_ref[:, k : k + 1] == expert, weights_ref[:, k : k + 1], 0.0)
    high = dense.astype(jnp.bfloat16).astype(jnp.float32)
    rest = dense - high
    middle = rest.astype(jnp.bfloat16).astype(jnp.float32)
    low = rest - middle
    terms = jnp.where(term == 0, high, jnp.where(term == 1, middle, low))
    out_ref[:, width:] = jnp.where(term < TERMS, terms, 0.0).astype(jnp.bfloat16)


def pack(hidden, ids, weights, experts):
    rows, width = hidden.shape
    extra = -(-experts * TERMS // LANES) * LANES
    return pl.pallas_call(
        lambda *refs: pack_kernel(experts, *refs),
        out_shape=jax.ShapeDtypeStruct((rows, width + extra), jnp.bfloat16),
        name="pack",
    )(hidden, ids, weights)


def expert_kernel(experts, pieces, chunk, me_ref, *refs):
    ins, (gate_w, up_w, down_w), outs = refs[:pieces], refs[pieces : pieces + 3], refs[pieces + 3 :]
    step, width = outs[0].shape
    info = jnp.concatenate([ref[:, width:] for ref in ins], axis=0).astype(jnp.float32)
    lane = lax.broadcasted_iota(jnp.int32, info.shape, 1)
    me = me_ref[0]
    mask = (lane == me) | (lane == me + experts) | (lane == me + 2 * experts)
    weight = jnp.sum(jnp.where(mask, info, 0.0), axis=1, keepdims=True)
    rows = jnp.concatenate([ref[:, :width] for ref in ins], axis=0)
    gate = jnp.dot(rows, gate_w[...], preferred_element_type=jnp.float32)
    up = jnp.dot(rows, up_w[...], preferred_element_type=jnp.float32)
    act = (gate / (1.0 + jnp.exp(-gate)) * up).astype(jnp.bfloat16)
    for k in range(width // chunk):
        part = slice(k * chunk, (k + 1) * chunk)
        value = jnp.dot(act, down_w[:, part], preferred_element_type=jnp.float32)
        value = (value * weight).astype(jnp.bfloat16)
        for p in range(pieces):
            outs[p][:, part] = value[p * step : (p + 1) * step]


def expert_values(pieces, weights, experts):
    step, packed = pieces[0].shape
    width, units = weights[0].shape
    rows = step * len(pieces)
    me = lax.axis_index("nodes").astype(jnp.int32).reshape(1)
    vmem = pl.BlockSpec(memory_space=pltpu.VMEM)
    fast = lambda w: pltpu.with_memory_space_constraint(w, pltpu.VMEM)
    return pl.pallas_call(
        lambda *refs: expert_kernel(experts, len(pieces), 512, *refs),
        out_shape=tuple(pltpu.VMEM((step, width), jnp.bfloat16) for _ in pieces),
        in_specs=[pl.BlockSpec(memory_space=pltpu.SMEM)] + [vmem] * (len(pieces) + 3),
        out_specs=tuple(vmem for _ in pieces),
        compiler_params=pltpu.CompilerParams(vmem_limit_bytes=12 * 1024 * 1024),
        cost_estimate=pl.CostEstimate(
            flops=2 * rows * width * units * 3,
            bytes_accessed=3 * width * units * 2 + 2 * rows * packed * 2,
            transcendentals=rows * units,
        ),
        name="expert",
    )(me, *(fast(p) for p in pieces), *(fast(w) for w in weights))


def load_kernel(gate_hbm, up_hbm, down_hbm, gate_out, up_out, down_out, sems):
    pairs = ((gate_hbm, gate_out), (up_hbm, up_out), (down_hbm, down_out))
    copies = [pltpu.make_async_copy(a, b, sems.at[i]) for i, (a, b) in enumerate(pairs)]
    for copy in copies:
        copy.start()
    for copy in copies:
        copy.wait()


def load(*matrices):
    size = sum(m.size * m.dtype.itemsize for m in matrices)
    return pl.pallas_call(
        load_kernel,
        out_shape=tuple(pltpu.VMEM(m.shape, m.dtype) for m in matrices),
        in_specs=[pl.BlockSpec(memory_space=pltpu.HBM)] * len(matrices),
        out_specs=tuple(pl.BlockSpec(memory_space=pltpu.VMEM) for _ in matrices),
        scratch_shapes=[pltpu.SemaphoreType.DMA((len(matrices),))],
        compiler_params=pltpu.CompilerParams(vmem_limit_bytes=1024 * 1024),
        cost_estimate=pl.CostEstimate(flops=0, bytes_accessed=2 * size, transcendentals=0),
        name="load",
    )(*(pltpu.with_memory_space_constraint(m, pltpu.HBM) for m in matrices))


def flip(x, masks):
    axes = ("nodes", "local")
    core = lax.axis_size("local")
    count = core * lax.axis_size("nodes")
    return lax.ppermute(x, axes, [(i, i ^ masks[bool(i & core)]) for i in range(count)])


def add(*terms):
    total = terms[0].astype(jnp.float32)
    for term in terms[1:]:
        total = total + term.astype(jnp.float32)
    return total


def routed_layer(hidden, ids, weights, w_gate, w_up, w_down):
    width = hidden.shape[1]
    core, nodes = lax.axis_size("local"), lax.axis_size("nodes")
    experts = w_gate.shape[0] * nodes
    far_bit = core * nodes // 2
    cube = [1 << k for k in range((core * nodes).bit_length() - 1) if (1 << k) not in (core, far_bit)]
    turn = lambda k: cube[k:] + cube[:k]
    near_steps = list(zip(turn(0), turn(1)))
    far_steps = list(zip(turn(2), turn(0)))
    sibling, across = (core, core), (far_bit, far_bit)

    packed = pack(hidden, ids, weights, experts)
    loaded = load(w_gate[0], w_up[0], w_down[0])

    def gather(held, steps):
        for masks in steps[:-1]:
            held = jnp.concatenate([held, flip(held, masks)], axis=0)
        return held, flip(held, steps[-1])

    def scatter(low, high, from_low, from_high, steps):
        sent = flip(add(high, flip(from_high, sibling)).astype(jnp.bfloat16), steps[-1])
        held = add(low, flip(from_low, sibling), sent)
        for masks in steps[-2::-1]:
            half = held.shape[0] // 2
            sent = flip(held[half:].astype(jnp.bfloat16), masks)
            held = add(held[:half], sent)
        return held

    far = flip(packed, across)
    results = []
    for held, steps in ((packed, near_steps), (far, far_steps)):
        low, high = gather(held, steps)
        pieces = (low, high, flip(low, sibling), flip(high, sibling))
        results.append(scatter(*expert_values(pieces, loaded, experts), steps))
    near, far = results
    return add(near, flip(far.astype(jnp.bfloat16), across)).astype(jnp.bfloat16)


def on_device(hidden_in, queries, cache, lengths, expert_ids, gate_weights, w_gate, w_up, w_down):
    expert_out = routed_layer(hidden_in, expert_ids, gate_weights, w_gate, w_up, w_down)
    context = attend(queries, cache, lengths)
    return (context, expert_out)


def solution(mesh):
    every = ("groups", "nodes", "local")
    return jax.shard_map(
        on_device,
        mesh=mesh,
        in_specs=(
            P(every, None),
            P(every, None, None),
            P(every, None, None),
            P(every),
            P(every, None),
            P(every, None),
            P("nodes", None, "local"),
            P("nodes", None, "local"),
            P("nodes", "local", None),
        ),
        out_specs=(P(every, None), P(every, None)),
        check_vma=False,
    )
```

```python
import jax
import jax.numpy as jnp
from jax import lax
from jax.experimental import pallas as pl
from jax.experimental.pallas import tpu as pltpu
from jax.sharding import PartitionSpec as P

LATENT = 512
LANES = 128
TERMS = 3

softmax_scale = 0.0722


def attend(queries, cache, lengths):
    scores = (
        jnp.einsum("bhd,btd->bht", queries, cache, preferred_element_type=jnp.float32)
        * softmax_scale
    )
    valid = lax.broadcasted_iota(jnp.int32, (1, 1, cache.shape[1]), 2) < lengths[:, None, None]
    scores = jnp.where(valid, scores, -1e30)
    highest = jnp.max(scores, axis=-1, keepdims=True)
    expo = jnp.exp(scores - highest)
    probs = (expo / jnp.sum(expo, axis=-1, keepdims=True)).astype(jnp.bfloat16)
    context = jnp.einsum(
        "bht,btc->bhc", probs, cache[:, :, :LATENT], preferred_element_type=jnp.float32
    )
    return context.astype(jnp.bfloat16).reshape(queries.shape[0], queries.shape[1] * LATENT)


def pack_kernel(experts, hidden_ref, ids_ref, weights_ref, out_ref):
    rows, width = hidden_ref.shape
    extra = out_ref.shape[1] - width
    out_ref[:, :width] = hidden_ref[...]
    lane = lax.broadcasted_iota(jnp.int32, (rows, extra), 1)
    expert, term = lane % experts, lane // experts
    dense = jnp.zeros((rows, extra), jnp.float32)
    for k in range(ids_ref.shape[1]):
        dense = dense + jnp.where(ids_ref[:, k : k + 1] == expert, weights_ref[:, k : k + 1], 0.0)
    high = dense.astype(jnp.bfloat16).astype(jnp.float32)
    rest = dense - high
    middle = rest.astype(jnp.bfloat16).astype(jnp.float32)
    low = rest - middle
    terms = jnp.where(term == 0, high, jnp.where(term == 1, middle, low))
    out_ref[:, width:] = jnp.where(term < TERMS, terms, 0.0).astype(jnp.bfloat16)


def pack(hidden, ids, weights, experts):
    rows, width = hidden.shape
    extra = -(-experts * TERMS // LANES) * LANES
    return pl.pallas_call(
        lambda *refs: pack_kernel(experts, *refs),
        out_shape=pltpu.VMEM((rows, width + extra), jnp.bfloat16),
        name="pack",
    )(hidden, ids, weights)


def expert_kernel(experts, pieces, chunk, me_ref, *refs):
    ins, (gate_w, up_w, down_w), outs = refs[:pieces], refs[pieces : pieces + 3], refs[pieces + 3 :]
    step, width = outs[0].shape
    info = jnp.concatenate([ref[:, width:] for ref in ins], axis=0).astype(jnp.float32)
    lane = lax.broadcasted_iota(jnp.int32, info.shape, 1)
    me = me_ref[0]
    mask = (lane == me) | (lane == me + experts) | (lane == me + 2 * experts)
    weight = jnp.sum(jnp.where(mask, info, 0.0), axis=1, keepdims=True)
    rows = jnp.concatenate([ref[:, :width] for ref in ins], axis=0)
    gate = jnp.dot(rows, gate_w[...], preferred_element_type=jnp.float32)
    up = jnp.dot(rows, up_w[...], preferred_element_type=jnp.float32)
    act = (gate / (1.0 + jnp.exp(-gate)) * up).astype(jnp.bfloat16)
    for k in range(width // chunk):
        part = slice(k * chunk, (k + 1) * chunk)
        value = jnp.dot(act, down_w[:, part], preferred_element_type=jnp.float32)
        value = (value * weight).astype(jnp.bfloat16)
        for p in range(pieces):
            outs[p][:, part] = value[p * step : (p + 1) * step]


def expert_values(pieces, weights, experts):
    step, packed = pieces[0].shape
    width, units = weights[0].shape
    rows = step * len(pieces)
    me = lax.axis_index("nodes").astype(jnp.int32).reshape(1)
    vmem = pl.BlockSpec(memory_space=pltpu.VMEM)
    fast = lambda w: pltpu.with_memory_space_constraint(w, pltpu.VMEM)
    return pl.pallas_call(
        lambda *refs: expert_kernel(experts, len(pieces), 512, *refs),
        out_shape=tuple(pltpu.VMEM((step, width), jnp.bfloat16) for _ in pieces),
        in_specs=[pl.BlockSpec(memory_space=pltpu.SMEM)] + [vmem] * (len(pieces) + 3),
        out_specs=tuple(vmem for _ in pieces),
        compiler_params=pltpu.CompilerParams(vmem_limit_bytes=12 * 1024 * 1024),
        cost_estimate=pl.CostEstimate(
            flops=2 * rows * width * units * 3,
            bytes_accessed=3 * width * units * 2 + 2 * rows * packed * 2,
            transcendentals=rows * units,
        ),
        name="expert",
    )(me, *(fast(p) for p in pieces), *(fast(w) for w in weights))


def load_kernel(source, target, sem):
    copy = pltpu.make_async_copy(source, target, sem)
    copy.start()
    copy.wait()


def load(matrix, after):
    matrix, _ = lax.optimization_barrier((matrix, after))
    size = matrix.size * matrix.dtype.itemsize
    return pl.pallas_call(
        load_kernel,
        out_shape=pltpu.VMEM(matrix.shape, matrix.dtype),
        in_specs=[pl.BlockSpec(memory_space=pltpu.HBM)],
        out_specs=pl.BlockSpec(memory_space=pltpu.VMEM),
        scratch_shapes=[pltpu.SemaphoreType.DMA],
        compiler_params=pltpu.CompilerParams(vmem_limit_bytes=1024 * 1024),
        cost_estimate=pl.CostEstimate(flops=0, bytes_accessed=2 * size, transcendentals=0),
        name="load",
    )(pltpu.with_memory_space_constraint(matrix, pltpu.HBM))


def flip(x, masks):
    axes = ("nodes", "local")
    core = lax.axis_size("local")
    count = core * lax.axis_size("nodes")
    return lax.ppermute(x, axes, [(i, i ^ masks[bool(i & core)]) for i in range(count)])


def add(*terms):
    total = terms[0].astype(jnp.float32)
    for term in terms[1:]:
        total = total + term.astype(jnp.float32)
    return total


def routed_layer(hidden, ids, weights, w_gate, w_up, w_down):
    width = hidden.shape[1]
    core, nodes = lax.axis_size("local"), lax.axis_size("nodes")
    experts = w_gate.shape[0] * nodes
    far_bit = core * nodes // 2
    cube = [1 << k for k in range((core * nodes).bit_length() - 1) if (1 << k) not in (core, far_bit)]
    turn = lambda k: cube[k:] + cube[:k]
    near_steps = list(zip(turn(0), turn(1)))
    far_steps = list(zip(turn(2), turn(0)))
    sibling, across = (core, core), (far_bit, far_bit)

    packed = pack(hidden, ids, weights, experts)

    def gather(held, steps, beside=None):
        for masks in steps[:-1]:
            sent = flip(held, masks)
            if beside is not None and masks == steps[-2]:
                beside = load(beside, held)
                sent, beside = lax.optimization_barrier((sent, beside))
            held = jnp.concatenate([held, sent], axis=0)
        return held, flip(held, steps[-1]), beside

    def scatter(low, high, from_low, from_high, steps):
        sent = flip(add(high, flip(from_high, sibling)).astype(jnp.bfloat16), steps[-1])
        held = add(low, flip(from_low, sibling), sent)
        for masks in steps[-2::-1]:
            half = held.shape[0] // 2
            sent = flip(held[half:].astype(jnp.bfloat16), masks)
            held = add(held[:half], sent)
        return held

    far = flip(packed, across)
    near_low, near_high, _ = gather(packed, near_steps)
    far_low, far_high, gate = gather(far, far_steps, w_gate[0])
    up, down = load(w_up[0], far_low), load(w_down[0], far_low)
    far_high, up, down = lax.optimization_barrier((far_high, up, down))
    loaded = (gate, up, down)
    results = []
    for low, high, steps in ((near_low, near_high, near_steps), (far_low, far_high, far_steps)):
        pieces = (low, high, flip(low, sibling), flip(high, sibling))
        results.append(scatter(*expert_values(pieces, loaded, experts), steps))
    near, far = results
    return add(near, flip(far.astype(jnp.bfloat16), across)).astype(jnp.bfloat16)


def on_device(hidden_in, queries, cache, lengths, expert_ids, gate_weights, w_gate, w_up, w_down):
    expert_out = routed_layer(hidden_in, expert_ids, gate_weights, w_gate, w_up, w_down)
    context = attend(queries, cache, lengths)
    return (context, expert_out)


def solution(mesh):
    every = ("groups", "nodes", "local")
    return jax.shard_map(
        on_device,
        mesh=mesh,
        in_specs=(
            P(every, None),
            P(every, None, None),
            P(every, None, None),
            P(every),
            P(every, None),
            P(every, None),
            P("nodes", None, "local"),
            P("nodes", None, "local"),
            P("nodes", "local", None),
        ),
        out_specs=(P(every, None), P(every, None)),
        check_vma=False,
    )
```

```python
import jax
import jax.numpy as jnp
from jax import lax
from jax.experimental import pallas as pl
from jax.experimental.pallas import tpu as pltpu
from jax.sharding import PartitionSpec as P

LATENT = 512
LANES = 128
TERMS = 3

softmax_scale = 0.0722


def attend(queries, cache, lengths):
    scores = (
        jnp.einsum("bhd,btd->bht", queries, cache, preferred_element_type=jnp.float32)
        * softmax_scale
    )
    valid = lax.broadcasted_iota(jnp.int32, (1, 1, cache.shape[1]), 2) < lengths[:, None, None]
    scores = jnp.where(valid, scores, -1e30)
    highest = jnp.max(scores, axis=-1, keepdims=True)
    expo = jnp.exp(scores - highest)
    probs = (expo / jnp.sum(expo, axis=-1, keepdims=True)).astype(jnp.bfloat16)
    context = jnp.einsum(
        "bht,btc->bhc", probs, cache[:, :, :LATENT], preferred_element_type=jnp.float32
    )
    return context.astype(jnp.bfloat16).reshape(queries.shape[0], queries.shape[1] * LATENT)


def pack_kernel(experts, hidden_ref, ids_ref, weights_ref, out_ref):
    rows, width = hidden_ref.shape
    extra = out_ref.shape[1] - width
    out_ref[:, :width] = hidden_ref[...]
    lane = lax.broadcasted_iota(jnp.int32, (rows, extra), 1)
    expert, term = lane % experts, lane // experts
    dense = jnp.zeros((rows, extra), jnp.float32)
    for k in range(ids_ref.shape[1]):
        dense = dense + jnp.where(ids_ref[:, k : k + 1] == expert, weights_ref[:, k : k + 1], 0.0)
    high = dense.astype(jnp.bfloat16).astype(jnp.float32)
    rest = dense - high
    middle = rest.astype(jnp.bfloat16).astype(jnp.float32)
    low = rest - middle
    terms = jnp.where(term == 0, high, jnp.where(term == 1, middle, low))
    out_ref[:, width:] = jnp.where(term < TERMS, terms, 0.0).astype(jnp.bfloat16)


def pack(hidden, ids, weights, experts):
    rows, width = hidden.shape
    extra = -(-experts * TERMS // LANES) * LANES
    return pl.pallas_call(
        lambda *refs: pack_kernel(experts, *refs),
        out_shape=pltpu.VMEM((rows, width + extra), jnp.bfloat16),
        name="pack",
    )(hidden, ids, weights)


def expert_kernel(experts, pieces, fetch, chunk, me_ref, *refs):
    ins, (gate_w, up_w, down_in), outs = refs[:pieces], refs[pieces : pieces + 3], refs[pieces + 3 :]
    step, width = outs[0].shape
    down_w = down_in
    if fetch:
        down_w, sem = outs[pieces:]
        copy = pltpu.make_async_copy(down_in, down_w, sem)
        copy.start()
    info = jnp.concatenate([ref[:, width:] for ref in ins], axis=0).astype(jnp.float32)
    lane = lax.broadcasted_iota(jnp.int32, info.shape, 1)
    me = me_ref[0]
    mask = (lane == me) | (lane == me + experts) | (lane == me + 2 * experts)
    weight = jnp.sum(jnp.where(mask, info, 0.0), axis=1, keepdims=True)
    rows = jnp.concatenate([ref[:, :width] for ref in ins], axis=0)
    gate = jnp.dot(rows, gate_w[...], preferred_element_type=jnp.float32)
    up = jnp.dot(rows, up_w[...], preferred_element_type=jnp.float32)
    act = (gate / (1.0 + jnp.exp(-gate)) * up).astype(jnp.bfloat16)
    if fetch:
        copy.wait()
    for k in range(width // chunk):
        part = slice(k * chunk, (k + 1) * chunk)
        value = jnp.dot(act, down_w[:, part], preferred_element_type=jnp.float32)
        value = (value * weight).astype(jnp.bfloat16)
        for p in range(pieces):
            outs[p][:, part] = value[p * step : (p + 1) * step]


def expert_values(pieces, weights, experts, fetch):
    step, packed = pieces[0].shape
    width, units = weights[0].shape
    rows = step * len(pieces)
    me = lax.axis_index("nodes").astype(jnp.int32).reshape(1)
    vmem = pl.BlockSpec(memory_space=pltpu.VMEM)
    fast = lambda w: pltpu.with_memory_space_constraint(w, pltpu.VMEM)
    down = weights[2]
    outs = [pltpu.VMEM((step, width), jnp.bfloat16) for _ in pieces]
    if fetch:
        outs.append(pltpu.VMEM(down.shape, down.dtype))
        down, place = pltpu.with_memory_space_constraint(down, pltpu.HBM), pl.BlockSpec(memory_space=pltpu.HBM)
    else:
        down, place = fast(down), vmem
    results = pl.pallas_call(
        lambda *refs: expert_kernel(experts, len(pieces), fetch, 512, *refs),
        out_shape=tuple(outs),
        in_specs=[pl.BlockSpec(memory_space=pltpu.SMEM)] + [vmem] * (len(pieces) + 2) + [place],
        out_specs=tuple(vmem for _ in outs),
        scratch_shapes=[pltpu.SemaphoreType.DMA] if fetch else [],
        compiler_params=pltpu.CompilerParams(vmem_limit_bytes=12 * 1024 * 1024),
        cost_estimate=pl.CostEstimate(
            flops=2 * rows * width * units * 3,
            bytes_accessed=3 * width * units * 2 + 2 * rows * packed * 2,
            transcendentals=rows * units,
        ),
        name="expert",
    )(me, *(fast(p) for p in pieces), fast(weights[0]), fast(weights[1]), down)
    return results[: len(pieces)], results[-1]


def load_kernel(*refs):
    count = len(refs) // 2
    copies = [pltpu.make_async_copy(refs[i], refs[count + i], refs[-1].at[i]) for i in range(count)]
    for copy in copies:
        copy.start()
    for copy in copies:
        copy.wait()


def load(*matrices):
    size = sum(m.size * m.dtype.itemsize for m in matrices)
    return pl.pallas_call(
        load_kernel,
        out_shape=tuple(pltpu.VMEM(m.shape, m.dtype) for m in matrices),
        in_specs=[pl.BlockSpec(memory_space=pltpu.HBM)] * len(matrices),
        out_specs=tuple(pl.BlockSpec(memory_space=pltpu.VMEM) for _ in matrices),
        scratch_shapes=[pltpu.SemaphoreType.DMA((len(matrices),))],
        compiler_params=pltpu.CompilerParams(vmem_limit_bytes=1024 * 1024),
        cost_estimate=pl.CostEstimate(flops=0, bytes_accessed=2 * size, transcendentals=0),
        name="load",
    )(*(pltpu.with_memory_space_constraint(m, pltpu.HBM) for m in matrices))


def flip(x, masks):
    axes = ("nodes", "local")
    core = lax.axis_size("local")
    count = core * lax.axis_size("nodes")
    return lax.ppermute(x, axes, [(i, i ^ masks[bool(i & core)]) for i in range(count)])


def add(*terms):
    total = terms[0].astype(jnp.float32)
    for term in terms[1:]:
        total = total + term.astype(jnp.float32)
    return total


def routed_layer(hidden, ids, weights, w_gate, w_up, w_down):
    width = hidden.shape[1]
    core, nodes = lax.axis_size("local"), lax.axis_size("nodes")
    experts = w_gate.shape[0] * nodes
    far_bit = core * nodes // 2
    cube = [1 << k for k in range((core * nodes).bit_length() - 1) if (1 << k) not in (core, far_bit)]
    shared, rest = cube[1], cube[:1] + cube[2:]
    near_steps = list(zip(rest + [shared], rest[1:] + rest[:1] + [shared]))
    far_steps = list(zip(cube, cube[1:] + cube[:1]))
    sibling, across = (core, core), (far_bit, far_bit)

    packed = pack(hidden, ids, weights, experts)

    def gather(held, steps):
        for masks in steps[:-1]:
            held = jnp.concatenate([held, flip(held, masks)], axis=0)
        return held, flip(held, steps[-1])

    def scatter(low, high, from_low, from_high, steps):
        sent = flip(add(high, flip(from_high, sibling)).astype(jnp.bfloat16), steps[-1])
        held = add(low, flip(from_low, sibling), sent)
        for masks in steps[-2::-1]:
            half = held.shape[0] // 2
            sent = flip(held[half:].astype(jnp.bfloat16), masks)
            held = add(held[:half], sent)
        return held

    far = flip(packed, across)
    far_low, far_high = gather(far, far_steps)
    near_low, near_high = gather(packed, near_steps)
    w_gate, w_up, w_down, _ = lax.optimization_barrier((w_gate[0], w_up[0], w_down[0], far_low))
    gate, up = load(w_gate, w_up)
    far_high, gate, up = lax.optimization_barrier((far_high, gate, up))

    pieces = (far_low, far_high, flip(far_low, sibling), flip(far_high, sibling))
    values, down = expert_values(pieces, (gate, up, w_down), experts, True)
    near_high, _ = lax.optimization_barrier((near_high, values[1]))
    far = scatter(*values, far_steps)
    pieces = (near_low, near_high, flip(near_low, sibling), flip(near_high, sibling))
    values, _ = expert_values(pieces, (gate, up, down), experts, False)
    near = scatter(*values, near_steps)
    return add(near, flip(far.astype(jnp.bfloat16), across)).astype(jnp.bfloat16)


def on_device(hidden_in, queries, cache, lengths, expert_ids, gate_weights, w_gate, w_up, w_down):
    expert_out = routed_layer(hidden_in, expert_ids, gate_weights, w_gate, w_up, w_down)
    context = attend(queries, cache, lengths)
    return (context, expert_out)


def solution(mesh):
    every = ("groups", "nodes", "local")
    return jax.shard_map(
        on_device,
        mesh=mesh,
        in_specs=(
            P(every, None),
            P(every, None, None),
            P(every, None, None),
            P(every),
            P(every, None),
            P(every, None),
            P("nodes", None, "local"),
            P("nodes", None, "local"),
            P("nodes", "local", None),
        ),
        out_specs=(P(every, None), P(every, None)),
        check_vma=False,
    )
```

```python
import jax
import jax.numpy as jnp
from jax import lax
from jax.experimental import pallas as pl
from jax.experimental.pallas import tpu as pltpu
from jax.sharding import PartitionSpec as P

LATENT = 512
LANES = 128
TERMS = 3

softmax_scale = 0.0722


def attend(queries, cache, lengths):
    scores = (
        jnp.einsum("bhd,btd->bht", queries, cache, preferred_element_type=jnp.float32)
        * softmax_scale
    )
    valid = lax.broadcasted_iota(jnp.int32, (1, 1, cache.shape[1]), 2) < lengths[:, None, None]
    scores = jnp.where(valid, scores, -1e30)
    highest = jnp.max(scores, axis=-1, keepdims=True)
    expo = jnp.exp(scores - highest)
    probs = (expo / jnp.sum(expo, axis=-1, keepdims=True)).astype(jnp.bfloat16)
    context = jnp.einsum(
        "bht,btc->bhc", probs, cache[:, :, :LATENT], preferred_element_type=jnp.float32
    )
    return context.astype(jnp.bfloat16).reshape(queries.shape[0], queries.shape[1] * LATENT)


def pack_kernel(experts, hidden_ref, ids_ref, weights_ref, out_ref):
    rows, width = hidden_ref.shape
    extra = out_ref.shape[1] - width
    out_ref[:, :width] = hidden_ref[...]
    lane = lax.broadcasted_iota(jnp.int32, (rows, extra), 1)
    expert, term = lane % experts, lane // experts
    dense = jnp.zeros((rows, extra), jnp.float32)
    for k in range(ids_ref.shape[1]):
        dense = dense + jnp.where(ids_ref[:, k : k + 1] == expert, weights_ref[:, k : k + 1], 0.0)
    high = dense.astype(jnp.bfloat16).astype(jnp.float32)
    rest = dense - high
    middle = rest.astype(jnp.bfloat16).astype(jnp.float32)
    low = rest - middle
    terms = jnp.where(term == 0, high, jnp.where(term == 1, middle, low))
    out_ref[:, width:] = jnp.where(term < TERMS, terms, 0.0).astype(jnp.bfloat16)


def pack(hidden, ids, weights, experts):
    rows, width = hidden.shape
    extra = -(-experts * TERMS // LANES) * LANES
    return pl.pallas_call(
        lambda *refs: pack_kernel(experts, *refs),
        out_shape=pltpu.VMEM((rows, width + extra), jnp.bfloat16),
        name="pack",
    )(hidden, ids, weights)


def expert_kernel(experts, pieces, chunk, me_ref, *refs):
    ins, (gate_w, up_w, down_w), outs = refs[:pieces], refs[pieces : pieces + 3], refs[pieces + 3 :]
    step, width = outs[0].shape
    info = jnp.concatenate([ref[:, width:] for ref in ins], axis=0).astype(jnp.float32)
    lane = lax.broadcasted_iota(jnp.int32, info.shape, 1)
    me = me_ref[0]
    mask = (lane == me) | (lane == me + experts) | (lane == me + 2 * experts)
    weight = jnp.sum(jnp.where(mask, info, 0.0), axis=1, keepdims=True)
    rows = jnp.concatenate([ref[:, :width] for ref in ins], axis=0)
    gate = jnp.dot(rows, gate_w[...], preferred_element_type=jnp.float32)
    up = jnp.dot(rows, up_w[...], preferred_element_type=jnp.float32)
    act = (gate / (1.0 + jnp.exp(-gate)) * up).astype(jnp.bfloat16)
    for k in range(width // chunk):
        part = slice(k * chunk, (k + 1) * chunk)
        value = jnp.dot(act, down_w[:, part], preferred_element_type=jnp.float32)
        value = (value * weight).astype(jnp.bfloat16)
        for p in range(pieces):
            outs[p][:, part] = value[p * step : (p + 1) * step]


def expert_values(me, pieces, weights, experts):
    step, packed = pieces[0].shape
    width, units = weights[0].shape
    rows = step * len(pieces)
    vmem = pl.BlockSpec(memory_space=pltpu.VMEM)
    fast = lambda w: pltpu.with_memory_space_constraint(w, pltpu.VMEM)
    return pl.pallas_call(
        lambda *refs: expert_kernel(experts, len(pieces), 512, *refs),
        out_shape=tuple(pltpu.VMEM((step, width), jnp.bfloat16) for _ in pieces),
        in_specs=[pl.BlockSpec(memory_space=pltpu.SMEM)] + [vmem] * (len(pieces) + 3),
        out_specs=tuple(vmem for _ in pieces),
        compiler_params=pltpu.CompilerParams(vmem_limit_bytes=12 * 1024 * 1024),
        cost_estimate=pl.CostEstimate(
            flops=2 * rows * width * units * 3,
            bytes_accessed=3 * width * units * 2 + 2 * rows * packed * 2,
            transcendentals=rows * units,
        ),
        name="expert",
    )(me, *(fast(p) for p in pieces), *(fast(w) for w in weights))


def load_kernel(cuts, *refs):
    count = len(refs) // 2
    copies = []
    for i in range(count):
        rows = refs[i].shape[0] // cuts
        for k in range(cuts):
            part = pl.ds(k * rows, rows)
            copies.append(pltpu.make_async_copy(refs[i].at[part], refs[count + i].at[part], refs[-1].at[i, k]))
    for copy in copies:
        copy.start()
    for copy in copies:
        copy.wait()


def load(matrices, after):
    *matrices, _ = lax.optimization_barrier((*matrices, after))
    size = sum(m.size * m.dtype.itemsize for m in matrices)
    cuts = 1
    return pl.pallas_call(
        lambda *refs: load_kernel(cuts, *refs),
        out_shape=tuple(pltpu.VMEM(m.shape, m.dtype) for m in matrices),
        in_specs=[pl.BlockSpec(memory_space=pltpu.HBM)] * len(matrices),
        out_specs=tuple(pl.BlockSpec(memory_space=pltpu.VMEM) for _ in matrices),
        scratch_shapes=[pltpu.SemaphoreType.DMA((len(matrices), cuts))],
        compiler_params=pltpu.CompilerParams(vmem_limit_bytes=1024 * 1024),
        cost_estimate=pl.CostEstimate(flops=0, bytes_accessed=2 * size, transcendentals=0),
        name="load",
    )(*(pltpu.with_memory_space_constraint(m, pltpu.HBM) for m in matrices))


def flip(x, masks):
    axes = ("nodes", "local")
    core = lax.axis_size("local")
    count = core * lax.axis_size("nodes")
    return lax.ppermute(x, axes, [(i, i ^ masks[bool(i & core)]) for i in range(count)])


def add(*terms):
    total = terms[0].astype(jnp.float32)
    for term in terms[1:]:
        total = total + term.astype(jnp.float32)
    return total


def routed_layer(hidden, ids, weights, w_gate, w_up, w_down):
    width = hidden.shape[1]
    core, nodes = lax.axis_size("local"), lax.axis_size("nodes")
    experts = w_gate.shape[0] * nodes
    far_bit = core * nodes // 2
    cube = [1 << k for k in range((core * nodes).bit_length() - 1) if (1 << k) not in (core, far_bit)]
    turn = lambda k: cube[k:] + cube[:k]
    near_steps = list(zip(turn(1), turn(2)))
    far_steps = list(zip(turn(0), turn(1)))
    sibling, across = (core, core), (far_bit, far_bit)

    me = lax.axis_index("nodes").astype(jnp.int32).reshape(1)
    hidden, me = lax.optimization_barrier((hidden, me))
    packed = pack(hidden, ids, weights, experts)

    def gather(held, steps, beside=None):
        for masks in steps[:-1]:
            sent = flip(held, masks)
            if beside is not None and masks == steps[-2]:
                (beside,) = load((beside,), held)
                sent, beside = lax.optimization_barrier((sent, beside))
            held = jnp.concatenate([held, sent], axis=0)
        return held, flip(held, steps[-1]), beside

    def scatter(low, high, from_low, from_high, steps):
        sent = flip(add(high, flip(from_high, sibling)).astype(jnp.bfloat16), steps[-1])
        held = add(low, flip(from_low, sibling), sent)
        for masks in steps[-2::-1]:
            half = held.shape[0] // 2
            sent = flip(held[half:].astype(jnp.bfloat16), masks)
            held = add(held[:half], sent)
        return held

    far = flip(packed, across)
    near_low, near_high, _ = gather(packed, near_steps)
    far_low, far_high, gate = gather(far, far_steps, w_gate[0])
    up, down = load((w_up[0], w_down[0]), far_low)
    far_high, up, down = lax.optimization_barrier((far_high, up, down))
    loaded = (gate, up, down)
    results = []
    for low, high, steps in ((near_low, near_high, near_steps), (far_low, far_high, far_steps)):
        pieces = (low, high, flip(low, sibling), flip(high, sibling))
        results.append(scatter(*expert_values(me, pieces, loaded, experts), steps))
    near, far = results
    return add(near, flip(far.astype(jnp.bfloat16), across)).astype(jnp.bfloat16)


def on_device(hidden_in, queries, cache, lengths, expert_ids, gate_weights, w_gate, w_up, w_down):
    expert_out = routed_layer(hidden_in, expert_ids, gate_weights, w_gate, w_up, w_down)
    context = attend(queries, cache, lengths)
    return (context, expert_out)


def solution(mesh):
    every = ("groups", "nodes", "local")
    return jax.shard_map(
        on_device,
        mesh=mesh,
        in_specs=(
            P(every, None),
            P(every, None, None),
            P(every, None, None),
            P(every),
            P(every, None),
            P(every, None),
            P("nodes", None, "local"),
            P("nodes", None, "local"),
            P("nodes", "local", None),
        ),
        out_specs=(P(every, None), P(every, None)),
        check_vma=False,
    )
```

```python
import jax
import jax.numpy as jnp
from jax import lax
from jax.experimental import pallas as pl
from jax.experimental.pallas import tpu as pltpu
from jax.sharding import PartitionSpec as P

LATENT = 512
LANES = 128
TERMS = 3

softmax_scale = 0.0722


def attend(queries, cache, lengths):
    scores = (
        jnp.einsum("bhd,btd->bht", queries, cache, preferred_element_type=jnp.float32)
        * softmax_scale
    )
    valid = lax.broadcasted_iota(jnp.int32, (1, 1, cache.shape[1]), 2) < lengths[:, None, None]
    scores = jnp.where(valid, scores, -1e30)
    highest = jnp.max(scores, axis=-1, keepdims=True)
    expo = jnp.exp(scores - highest)
    probs = (expo / jnp.sum(expo, axis=-1, keepdims=True)).astype(jnp.bfloat16)
    context = jnp.einsum(
        "bht,btc->bhc", probs, cache[:, :, :LATENT], preferred_element_type=jnp.float32
    )
    return context.astype(jnp.bfloat16).reshape(queries.shape[0], queries.shape[1] * LATENT)


def pack_kernel(experts, hidden_ref, ids_ref, weights_ref, out_ref):
    rows, width = hidden_ref.shape
    extra = out_ref.shape[1] - width
    out_ref[:, :width] = hidden_ref[...]
    lane = lax.broadcasted_iota(jnp.int32, (rows, extra), 1)
    expert, term = lane % experts, lane // experts
    dense = jnp.zeros((rows, extra), jnp.float32)
    for k in range(ids_ref.shape[1]):
        dense = dense + jnp.where(ids_ref[:, k : k + 1] == expert, weights_ref[:, k : k + 1], 0.0)
    high = dense.astype(jnp.bfloat16).astype(jnp.float32)
    rest = dense - high
    middle = rest.astype(jnp.bfloat16).astype(jnp.float32)
    low = rest - middle
    terms = jnp.where(term == 0, high, jnp.where(term == 1, middle, low))
    out_ref[:, width:] = jnp.where(term < TERMS, terms, 0.0).astype(jnp.bfloat16)


def pack(hidden, ids, weights, experts):
    rows, width = hidden.shape
    extra = -(-experts * TERMS // LANES) * LANES
    return pl.pallas_call(
        lambda *refs: pack_kernel(experts, *refs),
        out_shape=pltpu.VMEM((rows, width + extra), jnp.bfloat16),
        name="pack",
    )(hidden, ids, weights)


def expert_kernel(experts, pieces, chunk, me_ref, *refs):
    ins, (gate_w, up_w, down_w), outs = refs[:pieces], refs[pieces : pieces + 3], refs[pieces + 3 :]
    step, width = outs[0].shape
    info = jnp.concatenate([ref[:, width:] for ref in ins], axis=0).astype(jnp.float32)
    lane = lax.broadcasted_iota(jnp.int32, info.shape, 1)
    me = me_ref[0]
    mask = (lane == me) | (lane == me + experts) | (lane == me + 2 * experts)
    weight = jnp.sum(jnp.where(mask, info, 0.0), axis=1, keepdims=True)
    rows = jnp.concatenate([ref[:, :width] for ref in ins], axis=0)
    gate = jnp.dot(rows, gate_w[...], preferred_element_type=jnp.float32)
    up = jnp.dot(rows, up_w[...], preferred_element_type=jnp.float32)
    act = (gate / (1.0 + jnp.exp(-gate)) * up).astype(jnp.bfloat16)
    for k in range(width // chunk):
        part = slice(k * chunk, (k + 1) * chunk)
        value = jnp.dot(act, down_w[:, part], preferred_element_type=jnp.float32)
        value = (value * weight).astype(jnp.bfloat16)
        for p in range(pieces):
            outs[p][:, part] = value[p * step : (p + 1) * step]


def expert_values(me, pieces, weights, experts):
    step, packed = pieces[0].shape
    width, units = weights[0].shape
    rows = step * len(pieces)
    vmem = pl.BlockSpec(memory_space=pltpu.VMEM)
    fast = lambda w: pltpu.with_memory_space_constraint(w, pltpu.VMEM)
    return pl.pallas_call(
        lambda *refs: expert_kernel(experts, len(pieces), 512, *refs),
        out_shape=tuple(pltpu.VMEM((step, width), jnp.bfloat16) for _ in pieces),
        in_specs=[pl.BlockSpec(memory_space=pltpu.SMEM)] + [vmem] * (len(pieces) + 3),
        out_specs=tuple(vmem for _ in pieces),
        compiler_params=pltpu.CompilerParams(vmem_limit_bytes=12 * 1024 * 1024),
        cost_estimate=pl.CostEstimate(
            flops=2 * rows * width * units * 3,
            bytes_accessed=3 * width * units * 2 + 2 * rows * packed * 2,
            transcendentals=rows * units,
        ),
        name="expert",
    )(me, *(fast(p) for p in pieces), *(fast(w) for w in weights))


def load_kernel(cuts, *refs):
    count = len(refs) // 2
    copies = []
    for i in range(count):
        rows = refs[i].shape[0] // cuts
        for k in range(cuts):
            part = pl.ds(k * rows, rows)
            copies.append(pltpu.make_async_copy(refs[i].at[part], refs[count + i].at[part], refs[-1].at[i, k]))
    for copy in copies:
        copy.start()
    for copy in copies:
        copy.wait()


def load(matrices, after):
    *matrices, _ = lax.optimization_barrier((*matrices, after))
    size = sum(m.size * m.dtype.itemsize for m in matrices)
    cuts = 1
    return pl.pallas_call(
        lambda *refs: load_kernel(cuts, *refs),
        out_shape=tuple(pltpu.VMEM(m.shape, m.dtype) for m in matrices),
        in_specs=[pl.BlockSpec(memory_space=pltpu.HBM)] * len(matrices),
        out_specs=tuple(pl.BlockSpec(memory_space=pltpu.VMEM) for _ in matrices),
        scratch_shapes=[pltpu.SemaphoreType.DMA((len(matrices), cuts))],
        compiler_params=pltpu.CompilerParams(vmem_limit_bytes=1024 * 1024),
        cost_estimate=pl.CostEstimate(flops=0, bytes_accessed=2 * size, transcendentals=0),
        name="load",
    )(*(pltpu.with_memory_space_constraint(m, pltpu.HBM) for m in matrices))


def flip(x, masks):
    axes = ("nodes", "local")
    core = lax.axis_size("local")
    count = core * lax.axis_size("nodes")
    return lax.ppermute(x, axes, [(i, i ^ masks[bool(i & core)]) for i in range(count)])


def add(*terms):
    total = terms[0].astype(jnp.float32)
    for term in terms[1:]:
        total = total + term.astype(jnp.float32)
    return total


def routed_layer(hidden, ids, weights, w_gate, w_up, w_down):
    width = hidden.shape[1]
    core, nodes = lax.axis_size("local"), lax.axis_size("nodes")
    experts = w_gate.shape[0] * nodes
    far_bit = core * nodes // 2
    cube = [1 << k for k in range((core * nodes).bit_length() - 1) if (1 << k) not in (core, far_bit)]
    turn = lambda k: cube[k:] + cube[:k]
    near_steps = list(zip(turn(1), turn(2)))
    far_steps = list(zip(turn(0), turn(1)))
    sibling, across = (core, core), (far_bit, far_bit)

    me = lax.axis_index("nodes").astype(jnp.int32).reshape(1)
    hidden, me = lax.optimization_barrier((hidden, me))
    packed = pack(hidden, ids, weights, experts)

    def gather(held, steps, matrices=()):
        loaded = []
        for k, masks in enumerate(steps):
            sent = flip(held, masks)
            place = k - len(steps) + len(matrices)
            if matrices and place >= 0:
                (matrix,) = load((matrices[place],), held)
                sent, matrix = lax.optimization_barrier((sent, matrix))
                loaded.append(matrix)
            if masks != steps[-1]:
                held = jnp.concatenate([held, sent], axis=0)
        return held, sent, loaded

    def scatter(low, high, from_low, from_high, steps):
        high = add(high, flip(from_high, sibling)).astype(jnp.bfloat16)
        sent = flip(high, steps[-1])
        from_low, _ = lax.optimization_barrier((from_low, high))
        held = add(low, flip(from_low, sibling), sent)
        for masks in steps[-2::-1]:
            half = held.shape[0] // 2
            sent = flip(held[half:].astype(jnp.bfloat16), masks)
            held = add(held[:half], sent)
        return held

    far = flip(packed, across)
    near_low, near_high, _ = gather(packed, near_steps)
    far_low, far_high, loaded = gather(far, far_steps, (w_gate[0], w_up[0], w_down[0]))
    results = []
    for low, high, steps in ((near_low, near_high, near_steps), (far_low, far_high, far_steps)):
        pieces = (low, high, flip(low, sibling), flip(high, sibling))
        results.append(scatter(*expert_values(me, pieces, loaded, experts), steps))
    near, far = results
    return add(near, flip(far.astype(jnp.bfloat16), across)).astype(jnp.bfloat16)


def on_device(hidden_in, queries, cache, lengths, expert_ids, gate_weights, w_gate, w_up, w_down):
    expert_out = routed_layer(hidden_in, expert_ids, gate_weights, w_gate, w_up, w_down)
    context = attend(queries, cache, lengths)
    return (context, expert_out)


def solution(mesh):
    every = ("groups", "nodes", "local")
    return jax.shard_map(
        on_device,
        mesh=mesh,
        in_specs=(
            P(every, None),
            P(every, None, None),
            P(every, None, None),
            P(every),
            P(every, None),
            P(every, None),
            P("nodes", None, "local"),
            P("nodes", None, "local"),
            P("nodes", "local", None),
        ),
        out_specs=(P(every, None), P(every, None)),
        check_vma=False,
    )
```
